512 devices in a mesh: op: 64 (over z, y), sec: 8 (over x, core).
Axes of the slice: x: 4, y: 4, z: 16, core: 2. Of those that a mesh axis runs over, the one named last changes fastest.
Arguments:
- psi: bfloat16 [8, 384, 384], P('sec'), may hold values from -6 to 6
- left_ops: bfloat16 [3584, 384, 384], P(('op', 'sec')), may hold values from -0.3125 to 0.3125
- right_ops: bfloat16 [3584, 384, 384], P(('op', 'sec')), may hold values from -0.0234375 to 0.0234375
- term_src: int32 [3584], P(('op', 'sec')), may hold values from 0 to 7, as said below
- term_count: int32 [64, 8], P('op', 'sec'), may hold values from 1 to 7, as said below
Outputs:
- sigma: bfloat16 [8, 384, 384], P('sec')
The draws below stay inside these ranges and needn't reach their ends.
Inputs may be any that keep to these rules, and one draw needn't show every extreme that they name: `term_src`: the source sector of a slot of target sector g is g - 1, g or g + 1. `term_count`: at least one device has all 7 slots live in every draw.
All inputs are finite; a program needn't handle non-finite values.
Results may differ from the reference program's by a relative error of at most 0.0051.
Values may be sent and summed in bfloat16 or wider, within the bound.
A program may use at most 64 MiB of HBM per device.

```python
import jax
import jax.numpy as jnp
from jax import lax

M = 384
TERM_DEV = 7
SECTORS = 8
TERMS = 3584
N_OP = 64
N_SEC = 8


def draw_term_src(key, part):
    key = jax.random.fold_in(key, 11)
    slots = jnp.arange(TERMS, dtype=jnp.int32)
    target = slots // TERM_DEV % N_SEC
    offset = jax.random.randint(key, (TERMS,), -1, 2, dtype=jnp.int32)
    return jnp.clip(target + offset, 0, N_SEC - 1).astype(jnp.int32)


def draw_term_count(key, part):
    key = jax.random.fold_in(key, 23)
    key_a, key_b = jax.random.split(key)
    counts = 1 + jax.random.randint(key_a, (N_OP * N_SEC,), 0, min(4, TERM_DEV), dtype=jnp.int32)
    heavy = jax.random.randint(key_b, (), 0, N_OP * N_SEC, dtype=jnp.int32)
    counts = jnp.where(jnp.arange(N_OP * N_SEC, dtype=jnp.int32) == heavy, TERM_DEV, counts)
    return counts.reshape(N_OP, N_SEC).astype(jnp.int32)


def block_scale(rng, extent, cuts, smallest, top_value):
    loudness = 1.0
    for axis_at, parts in cuts:
        steps = jax.random.uniform(jax.random.fold_in(jax.random.fold_in(rng, 6), axis_at), (parts,), jnp.float32, smallest / len(cuts), top_value / len(cuts))
        loudness = loudness * jnp.repeat(jnp.exp(steps), extent[axis_at] // parts).reshape((-1,) + (1,) * (len(extent) - 1 - axis_at))
    return loudness


def centred(own_key, dims, width, reach, shards=(), held_as=jnp.bfloat16):
    factor_of = block_scale(own_key, dims, shards, -0.22, 0.18) if shards else 1.0
    drawn = jax.random.normal(own_key, dims, jnp.float32) * width * factor_of
    return jnp.minimum(jnp.maximum(drawn, -reach), reach).astype(held_as)


def setup_inputs(seed: int = 0) -> dict:
    key_list = jax.random.split(jax.random.key(seed), 6)
    return {
        "psi": centred(key_list[0], (SECTORS, M, M), 1.0, 6.0, ((0, 8),)),
        "left_ops": centred(key_list[1], (TERMS, M, M), M ** -0.5, 0.3125, ((0, 512),)),
        "right_ops": centred(key_list[2], (TERMS, M, M), (5 * M * N_OP // 2) ** -0.5, 0.0234375, ((0, 512),)),
        "term_src": draw_term_src(jax.random.fold_in(key_list[5], 71), 0),
        "term_count": draw_term_count(jax.random.fold_in(key_list[5], 71), 0),
    }


def reference(psi, left_ops, right_ops, term_src, term_count):
    psi_wide = psi.astype(jnp.float32)

    def add_term(acc, slot):
        device = slot // TERM_DEV
        op_index = device // SECTORS
        target = device % SECTORS
        count = term_count[op_index, target]
        live = (slot % TERM_DEV) < count

        def compute(acc):
            block = lax.dynamic_index_in_dim(psi_wide, term_src[slot], 0, keepdims=False)
            right = lax.dynamic_index_in_dim(right_ops, slot, 0, keepdims=False).astype(jnp.float32)
            left = lax.dynamic_index_in_dim(left_ops, slot, 0, keepdims=False).astype(jnp.float32)
            inner = jnp.dot(block, right).astype(jnp.bfloat16).astype(jnp.float32)
            term = jnp.dot(left, inner)
            return acc.at[target].add(term)

        return lax.cond(live, compute, lambda a: a, acc), None

    start = jnp.zeros((SECTORS, M, M), jnp.float32)
    total, unused = lax.scan(add_term, start, jnp.arange(TERMS, dtype=jnp.int32))
    return total.astype(jnp.bfloat16)
```

```python
import jax
import jax.numpy as jnp
from jax import lax
from jax.experimental import pallas as pl
from jax.experimental.pallas import tpu as pltpu
from jax.sharding import PartitionSpec as P

MESH = pl.DeviceIdType.MESH
NY, NZ, NSEC = 4, 16, 8
M, SLOTS = 384, 7
OWNERS, ROWS = 12, 8
FAR_FIRST = (8, 7, 9, 6, 10, 5, 11, 4, 12, 3, 13, 2, 14, 1, 15)
Y_FIRST = (2, 1, 3)


def kernel(
    psi, left, right, src, count, out,
    near, lbuf, rbuf, acc, pbuf, yrecv, zbuf, zrecv, quarter,
    psi_sem, l_sem, r_sem, psi_send, psi_recv,
    ys_sem, yr_sem, zs_sem, zr_sem, gs_sem, gr_sem, hs_sem, hr_sem, out_sem,
):
    op, sec = lax.axis_index("op"), lax.axis_index("sec")
    z, y = op // NY, op % NY

    def at_y(d):
        return (z * NY + (y + d) % NY, sec)

    def at_z(d):
        return ((z + d) % NZ * NY + y, sec)

    def at_sec(d):
        return (op, (sec + d) % NSEC)

    def remote(a, b, s, r, device):
        return pltpu.make_async_remote_copy(
            src_ref=a, dst_ref=b, send_sem=s, recv_sem=r,
            device_id=device, device_id_type=MESH,
        )

    own = pltpu.make_async_copy(psi.at[0], near.at[1], psi_sem)
    own.start()
    loads_r = [pltpu.make_async_copy(right.at[t], rbuf.at[t], r_sem.at[t]) for t in range(SLOTS)]
    loads_l = [pltpu.make_async_copy(left.at[t], lbuf.at[t], l_sem.at[t]) for t in range(SLOTS)]
    for t in range(SLOTS):
        loads_r[t].start()
        loads_l[t].start()

    peers = [at_sec(1), at_sec(-1)] + [at_y(d) for d in Y_FIRST] + [at_z(d) for d in FAR_FIRST]
    barrier = pltpu.get_barrier_semaphore()
    for peer in reversed(peers):
        pl.semaphore_signal(barrier, inc=1, device_id=peer, device_id_type=MESH)
    pl.semaphore_wait(barrier, len(peers))

    up = remote(psi.at[0], near.at[0], psi_send.at[0], psi_recv.at[0], at_sec(1))
    down = remote(psi.at[0], near.at[2], psi_send.at[1], psi_recv.at[1], at_sec(-1))
    up.start()
    down.start()
    own.wait()
    up.wait_recv()
    down.wait_recv()

    live = count[0, 0]
    for t in range(SLOTS):
        loads_r[t].wait()
        block = near[jnp.clip(src[t] - sec + 1, 0, 2)]
        inner = jnp.dot(block, rbuf[t], preferred_element_type=jnp.float32)
        inner = jnp.where(t < live, inner, 0.0).astype(jnp.bfloat16)
        loads_l[t].wait()
        term = jnp.dot(lbuf[t], inner, preferred_element_type=jnp.float32)
        term = term.reshape(NY, OWNERS, ROWS, M)
        if t == 0:
            acc[...] = term
        elif t < SLOTS - 1:
            acc[...] += term
        else:
            total = acc[...] + term
            acc[...] = total
            pbuf[...] = total.astype(jnp.bfloat16)

    copies = []
    for d in Y_FIRST:
        c = remote(pbuf.at[(y + d) % NY], yrecv.at[d - 1], ys_sem.at[d - 1], yr_sem.at[d - 1], at_y(d))
        c.start()
        copies.append(c)
    for c in copies:
        c.wait_recv()
    summed = acc[y]
    for d in range(1, NY):
        summed = summed + yrecv[d - 1].astype(jnp.float32)
    zbuf[...] = summed.astype(jnp.bfloat16)

    def piece(d):
        p = (z + d) % NZ
        return p < OWNERS, remote(zbuf.at[p % OWNERS], zrecv.at[d - 1], zs_sem.at[d - 1], zr_sem.at[d - 1], at_z(d))

    for d in FAR_FIRST:
        ok, c = piece(d)

        @pl.when(ok)
        def _():
            c.start()

    def spread(d):
        return remote(quarter.at[z % OWNERS], quarter.at[z % OWNERS], gs_sem.at[d - 1], gr_sem.at[z % OWNERS], at_z(d))

    @pl.when(z < OWNERS)
    def _():
        total = zbuf[z % OWNERS].astype(jnp.float32)
        for d in reversed(FAR_FIRST):
            piece(d)[1].wait_recv()
            total = total + zrecv[d - 1].astype(jnp.float32)
        quarter[z % OWNERS] = total.astype(jnp.bfloat16)
        for d in FAR_FIRST:
            spread(d).start()

    for p in range(OWNERS):
        @pl.when(p != z)
        def _():
            remote(quarter.at[p], quarter.at[p], gs_sem.at[0], gr_sem.at[p], at_z(1)).wait_recv()

    for d in Y_FIRST:
        c = remote(quarter, out.at[y], hs_sem.at[d - 1], hr_sem.at[d - 1], at_y(d))
        c.start()
        copies.append(c)
    mine = pltpu.make_async_copy(quarter, out.at[y], out_sem)
    mine.start()

    up.wait_send()
    down.wait_send()
    for c in copies[:3]:
        c.wait_send()
    for d in FAR_FIRST:
        ok, c = piece(d)

        @pl.when(ok)
        def _():
            c.wait_send()

    @pl.when(z < OWNERS)
    def _():
        for d in FAR_FIRST:
            spread(d).wait_send()

    mine.wait()
    for c in copies[3:]:
        c.wait()


def local(psi, left_ops, right_ops, term_src, term_count):
    hbm = pl.BlockSpec(memory_space=pl.ANY)
    smem = pl.BlockSpec(memory_space=pltpu.SMEM)
    dma = pltpu.SemaphoreType.DMA
    bf16, f32 = jnp.bfloat16, jnp.float32
    out = pl.pallas_call(
        kernel,
        out_shape=jax.ShapeDtypeStruct((NY, OWNERS, ROWS, M), bf16),
        in_specs=[hbm, hbm, hbm, smem, smem],
        out_specs=hbm,
        scratch_shapes=[
            pltpu.VMEM((3, M, M), bf16),
            pltpu.VMEM((SLOTS, M, M), bf16),
            pltpu.VMEM((SLOTS, M, M), bf16),
            pltpu.VMEM((NY, OWNERS, ROWS, M), f32),
            pltpu.VMEM((NY, OWNERS, ROWS, M), bf16),
            pltpu.VMEM((NY - 1, OWNERS, ROWS, M), bf16),
            pltpu.VMEM((OWNERS, ROWS, M), bf16),
            pltpu.VMEM((NZ - 1, ROWS, M), bf16),
            pltpu.VMEM((OWNERS, ROWS, M), bf16),
            dma, dma((SLOTS,)), dma((SLOTS,)), dma((2,)), dma((2,)),
            dma((NY - 1,)), dma((NY - 1,)),
            dma((NZ - 1,)), dma((NZ - 1,)),
            dma((NZ - 1,)), dma((OWNERS,)),
            dma((NY - 1,)), dma((NY - 1,)), dma,
        ],
        compiler_params=pltpu.CompilerParams(
            collective_id=0, has_side_effects=True, vmem_limit_bytes=60 * 1024 * 1024
        ),
        cost_estimate=pl.CostEstimate(
            flops=4 * SLOTS * M**3, bytes_accessed=4 * SLOTS * M * M, transcendentals=0
        ),
        name="sigma_sum",
    )(psi, left_ops, right_ops, term_src, term_count)
    return out.reshape(1, M, M)


def solution(mesh):
    in_specs = (
        P("sec", None, None),
        P(("op", "sec"), None, None),
        P(("op", "sec"), None, None),
        P(("op", "sec")),
        P("op", "sec"),
    )
    out_specs = P("sec", None, None)
    return jax.shard_map(local, mesh=mesh, in_specs=in_specs, out_specs=out_specs, check_vma=False)
```

```python
import jax
import jax.numpy as jnp
from jax import lax
from jax.experimental import pallas as pl
from jax.experimental.pallas import tpu as pltpu
from jax.sharding import PartitionSpec as P

MESH = pl.DeviceIdType.MESH
NY, NZ, NSEC = 4, 16, 8
M, SLOTS = 384, 7
NB, OWN, ROWS = 4, 3, 8
FAR_FIRST = (8, 7, 9, 6, 10, 5, 11, 4, 12, 3, 13, 2, 14, 1, 15)
FAR_BLOCKS = (2, 1, 3, 0)
Y_FIRST = (2, 1, 3)


def kernel(
    psi, left, right, src, count, out,
    near, lbuf, rbuf, icat, pbuf, yrecv, zbuf, zrecv, quarter,
    psi_sem, l_sem, r_sem, psi_send, psi_recv,
    ys_sem, yr_sem, zs_sem, zr_sem, gs_sem, gr_sem, hs_sem, hr_sem, out_sem,
    know_a, know_b, know_c,
):
    op, sec = lax.axis_index("op"), lax.axis_index("sec")
    z, y = op // NY, op % NY
    zb, zk = z // NB, z % NB

    def at_y(d):
        return (z * NY + (y + d) % NY, sec)

    def at_z(d):
        return ((z + d) % NZ * NY + y, sec)

    def at_sec(d):
        return (op, (sec + d) % NSEC)

    def remote(a, b, s, r, device):
        return pltpu.make_async_remote_copy(
            src_ref=a, dst_ref=b, send_sem=s, recv_sem=r,
            device_id=device, device_id_type=MESH,
        )

    def signal(sem, device):
        pl.semaphore_signal(sem, inc=1, device_id=device, device_id_type=MESH)

    barrier = pltpu.get_barrier_semaphore()
    beside = [at_z(1), at_z(-1), at_y(1), at_y(-1)]
    for peer in [at_sec(1), at_sec(-1)] + beside:
        signal(barrier, peer)

    own = pltpu.make_async_copy(psi.at[0], near.at[1], psi_sem)
    own.start()
    loads = []
    for t in range(SLOTS):
        loads.append(pltpu.make_async_copy(right.at[t], rbuf.at[t], r_sem.at[t]))
    for t in range(SLOTS):
        loads.append(pltpu.make_async_copy(left.at[t], lbuf.at[:, pl.ds(t * M, M)], l_sem.at[t]))
    for c in loads:
        c.start()

    pl.semaphore_wait(barrier, 6)
    up = remote(psi.at[0], near.at[0], psi_send.at[0], psi_recv.at[0], at_sec(1))
    down = remote(psi.at[0], near.at[2], psi_send.at[1], psi_recv.at[1], at_sec(-1))
    up.start()
    down.start()
    for peer in beside:
        signal(know_a, peer)
    own.wait()
    for c in loads:
        c.wait()
    pl.semaphore_wait(know_a, 4)
    for d in (2, -2):
        signal(know_b, at_z(d))
    up.wait_recv()
    down.wait_recv()

    live = count[0, 0]
    for t in range(SLOTS):
        block = near[jnp.clip(src[t] - sec + 1, 0, 2)]
        inner = jnp.dot(block, rbuf[t], preferred_element_type=jnp.float32)
        icat[pl.ds(t * M, M)] = jnp.where(t < live, inner, 0.0).astype(jnp.bfloat16)
    total = jnp.dot(lbuf[...], icat[...], preferred_element_type=jnp.float32)
    pbuf[...] = total.astype(jnp.bfloat16).reshape(NY, NB, OWN, ROWS, M)

    y_copies = []
    for e in FAR_BLOCKS:
        b = (zb + e) % NB
        row = []
        for d in Y_FIRST:
            c = remote(
                pbuf.at[(y + d) % NY, b], yrecv.at[d - 1, b],
                ys_sem.at[d - 1, e], yr_sem.at[d - 1, e], at_y(d),
            )
            c.start()
            row.append(c)
        y_copies.append(row)
    pl.semaphore_wait(know_b, 2)
    for d in (4, -4):
        signal(know_c, at_z(d))

    def piece(e, k):
        b = (zb + e) % NB
        owner = b * NB + k
        return remote(
            zbuf.at[b, k], zrecv.at[z], zs_sem.at[e, k], zr_sem.at[z], (owner * NY + y, sec)
        )

    for i, e in enumerate(FAR_BLOCKS):
        b = (zb + e) % NB
        for c in y_copies[i]:
            c.wait_recv()
        total = pbuf[y, b].astype(jnp.float32)
        for d in range(1, NY):
            total = total + yrecv[d - 1, b].astype(jnp.float32)
        zbuf[b] = total.astype(jnp.bfloat16)
        if i == 0:
            pl.semaphore_wait(know_c, 2)
        for k in range(OWN):
            if e == 0:
                @pl.when(k != zk)
                def _():
                    piece(e, k).start()
            else:
                piece(e, k).start()

    def spread(d):
        mine = quarter.at[zb, zk % OWN]
        return remote(mine, mine, gs_sem.at[d - 1], gr_sem.at[zb, zk % OWN], at_z(d))

    @pl.when(zk < OWN)
    def _():
        total = zbuf[zb, zk % OWN].astype(jnp.float32)
        for d in reversed(FAR_FIRST):
            s = (z + d) % NZ
            remote(zbuf.at[0, 0], zrecv.at[s], zs_sem.at[0, 0], zr_sem.at[s], at_z(1)).wait_recv()
            total = total + zrecv[s].astype(jnp.float32)
        quarter[zb, zk % OWN] = total.astype(jnp.bfloat16)
        for d in FAR_FIRST:
            spread(d).start()

    h_copies = []
    for e in reversed(FAR_BLOCKS):
        b = (zb + e) % NB
        for k in range(OWN):
            def arrived():
                part = quarter.at[b, k]
                remote(part, part, gs_sem.at[0], gr_sem.at[b, k], at_z(1)).wait_recv()

            if e == 0:
                pl.when(k != zk)(arrived)
            else:
                arrived()
        for d in Y_FIRST:
            c = remote(
                quarter.at[b], out.at[y, b], hs_sem.at[d - 1, e], hr_sem.at[d - 1, e], at_y(d)
            )
            c.start()
            h_copies.append(c)
        c = pltpu.make_async_copy(quarter.at[b], out.at[y, b], out_sem.at[e])
        c.start()
        h_copies.append(c)

    up.wait_send()
    down.wait_send()
    for row in y_copies:
        for c in row:
            c.wait_send()
    for e in FAR_BLOCKS:
        for k in range(OWN):
            if e == 0:
                @pl.when(k != zk)
                def _():
                    piece(e, k).wait_send()
            else:
                piece(e, k).wait_send()

    @pl.when(zk < OWN)
    def _():
        for d in FAR_FIRST:
            spread(d).wait_send()

    for c in h_copies:
        c.wait()


def local(psi, left_ops, right_ops, term_src, term_count):
    hbm = pl.BlockSpec(memory_space=pl.ANY)
    smem = pl.BlockSpec(memory_space=pltpu.SMEM)
    dma, plain = pltpu.SemaphoreType.DMA, pltpu.SemaphoreType.REGULAR
    bf16 = jnp.bfloat16
    out = pl.pallas_call(
        kernel,
        out_shape=jax.ShapeDtypeStruct((NY, NB, OWN, ROWS, M), bf16),
        in_specs=[hbm, hbm, hbm, smem, smem],
        out_specs=hbm,
        scratch_shapes=[
            pltpu.VMEM((3, M, M), bf16),
            pltpu.VMEM((M, SLOTS * M), bf16),
            pltpu.VMEM((SLOTS, M, M), bf16),
            pltpu.VMEM((SLOTS * M, M), bf16),
            pltpu.VMEM((NY, NB, OWN, ROWS, M), bf16),
            pltpu.VMEM((NY - 1, NB, OWN, ROWS, M), bf16),
            pltpu.VMEM((NB, OWN, ROWS, M), bf16),
            pltpu.VMEM((NZ, ROWS, M), bf16),
            pltpu.VMEM((NB, OWN, ROWS, M), bf16),
            dma, dma((SLOTS,)), dma((SLOTS,)), dma((2,)), dma((2,)),
            dma((NY - 1, NB)), dma((NY - 1, NB)),
            dma((NB, OWN)), dma((NZ,)),
            dma((NZ - 1,)), dma((NB, OWN)),
            dma((NY - 1, NB)), dma((NY - 1, NB)), dma((NB,)),
            plain, plain, plain,
        ],
        compiler_params=pltpu.CompilerParams(
            collective_id=0, has_side_effects=True, vmem_limit_bytes=60 * 1024 * 1024
        ),
        cost_estimate=pl.CostEstimate(
            flops=4 * SLOTS * M**3, bytes_accessed=4 * SLOTS * M * M, transcendentals=0
        ),
        name="sigma_sum",
    )(psi, left_ops, right_ops, term_src, term_count)
    return out.reshape(1, M, M)


def solution(mesh):
    in_specs = (
        P("sec", None, None),
        P(("op", "sec"), None, None),
        P(("op", "sec"), None, None),
        P(("op", "sec")),
        P("op", "sec"),
    )
    out_specs = P("sec", None, None)
    return jax.shard_map(local, mesh=mesh, in_specs=in_specs, out_specs=out_specs, check_vma=False)
```

```python
import jax
import jax.numpy as jnp
from jax import lax
from jax.experimental import pallas as pl
from jax.experimental.pallas import tpu as pltpu
from jax.sharding import PartitionSpec as P

MESH = pl.DeviceIdType.MESH
NY, NZ, NSEC = 4, 16, 8
M, SLOTS = 384, 7
PARTS = ((0, 256), (256, 128))
NB, OWN, ROWS, FIRST = 4, 3, 8, 10
NEAR_FIRST = (1, 15, 2, 14, 3, 13, 4, 12, 5, 11, 6, 10, 7, 9, 8)
FAR_BLOCKS = (
    (3, 2, 1, 0), (3, 2, 0, 1), (0, 3, 1, 2), (0, 1, 2, 3), (1, 0, 2, 3), (1, 2, 0, 3), (2, 1, 3, 0), (2, 3, 1, 0),
)
SPREAD = (0, 1, 2, 3, 4, 5, 6, 7, 15, 14, 13, 12, 8, 11, 9, 10)
Y_FIRST = (2, 1, 3)


def kernel(
    psi, left, right, src_in, count_in, out, src, count,
    near_a, near_b, lbuf, rbuf, icat, acc, pbuf, yrecv, zbuf, zrecv, quarter,
    psi_sem, l_sem, r_sem, psi_send, psi_recv,
    ys_sem, yr_sem, zs_sem, zr_sem, gs_sem, gr_sem, hs_sem, hr_sem, out_sem,
    know_a, know_b, know_c, scalar_sem,
):
    op, sec = lax.axis_index("op"), lax.axis_index("sec")
    z, y = op // NY, op % NY
    mine = (z + NZ - FIRST) % NZ
    is_owner = mine < NB * OWN
    mb, mk = mine // OWN % NB, mine % OWN
    group = jnp.where(is_owner, mine // OWN, mine - NB * OWN + NB)
    blocks = []
    for i in range(NB):
        block = FAR_BLOCKS[0][i]
        for g in range(1, 2 * NB):
            block = jnp.where(group == g, FAR_BLOCKS[g][i], block)
        blocks.append(block)

    def at_y(d):
        return (z * NY + (y + d) % NY, sec)

    def at_z(d):
        return ((z + d) % NZ * NY + y, sec)

    def at_sec(d):
        return (op, (sec + d) % NSEC)

    def remote(a, b, s, r, device):
        return pltpu.make_async_remote_copy(
            src_ref=a, dst_ref=b, send_sem=s, recv_sem=r,
            device_id=device, device_id_type=MESH,
        )

    def signal(sem, device):
        pl.semaphore_signal(sem, inc=1, device_id=device, device_id_type=MESH)

    barrier = pltpu.get_barrier_semaphore()
    beside = [at_z(1), at_z(-1), at_y(1), at_y(-1)]
    for peer in beside:
        signal(barrier, peer)
    has_up, has_down = sec < NSEC - 1, sec > 0

    @pl.when(has_up)
    def _():
        signal(barrier, at_sec(1))

    @pl.when(has_down)
    def _():
        signal(barrier, at_sec(-1))

    near = (near_a, near_b)
    own = [
        pltpu.make_async_copy(psi.at[0, pl.ds(*part)], near[p].at[1], psi_sem.at[p])
        for p, part in enumerate(PARTS)
    ]
    for c in own:
        c.start()
    loads = [
        pltpu.make_async_copy(src_in, src, scalar_sem.at[0]),
        pltpu.make_async_copy(count_in, count, scalar_sem.at[1]),
    ]
    for t in range(SLOTS):
        loads.append(pltpu.make_async_copy(right.at[t], rbuf.at[t], r_sem.at[t]))
    for p, (first, rows) in enumerate(PARTS):
        for t in range(SLOTS):
            loads.append(pltpu.make_async_copy(
                left.at[t, :, pl.ds(first, rows)],
                lbuf.at[:, pl.ds(SLOTS * first + t * rows, rows)],
                l_sem.at[p, t],
            ))

    ends = ((sec == 0) | (sec == NSEC - 1)).astype(jnp.int32)
    pl.semaphore_wait(barrier, 6 - ends)
    for c in own:
        c.wait()
    even = sec % 2 == 0
    up, down, fill_low, fill_high = [], [], [], []
    for p, part in enumerate(PARTS):
        rows, held = pl.ds(*part), near[p]
        up.append(remote(held.at[1], held.at[0], psi_send.at[p, 0], psi_recv.at[p, 0], at_sec(1)))
        down.append(remote(held.at[1], held.at[2], psi_send.at[p, 1], psi_recv.at[p, 1], at_sec(-1)))
        fill_low.append(pltpu.make_async_copy(psi.at[0, rows], held.at[0], psi_recv.at[p, 0]))
        fill_high.append(pltpu.make_async_copy(psi.at[0, rows], held.at[2], psi_recv.at[p, 1]))
    for p in range(len(PARTS)):
        pl.when(even & has_down)(down[p].start)
        pl.when(jnp.logical_not(even) & has_up)(up[p].start)
    for p in range(len(PARTS)):
        pl.when(even)(up[p].start)
        pl.when(jnp.logical_not(even))(down[p].start)
        pl.when(sec == 0)(fill_low[p].start)
        pl.when(sec == NSEC - 1)(fill_high[p].start)
    for peer in beside:
        signal(know_a, peer)
    for c in loads:
        c.start()
    pl.semaphore_wait(know_a, 4)
    for d in (2, -2):
        signal(know_b, at_z(d))
    for c in loads:
        c.wait()

    live = count[0, 0]
    for p, (first, rows) in enumerate(PARTS):
        pl.when(has_down)(up[p].wait_recv)
        pl.when(has_up)(down[p].wait_recv)
        pl.when(sec == 0)(fill_low[p].wait)
        pl.when(sec == NSEC - 1)(fill_high[p].wait)
        for t in range(SLOTS):
            block = near[p][jnp.clip(src[t] - sec + 1, 0, 2)]
            inner = jnp.dot(block, rbuf[t], preferred_element_type=jnp.float32)
            inner = jnp.where(t < live, inner, 0.0).astype(jnp.bfloat16)
            icat[pl.ds(SLOTS * first + t * rows, rows)] = inner
        span = pl.ds(SLOTS * first, SLOTS * rows)
        term = jnp.dot(lbuf[:, span], icat[span], preferred_element_type=jnp.float32)
        if p == 0:
            acc[...] = term
    total = acc[...] + term
    pbuf[...] = total.astype(jnp.bfloat16).reshape(NY, NB, OWN, ROWS, M)

    y_copies = []
    for i, b in enumerate(blocks):
        row = []
        for d in Y_FIRST:
            c = remote(
                pbuf.at[(y + d) % NY, b], yrecv.at[d - 1, b],
                ys_sem.at[d - 1, i], yr_sem.at[d - 1, i], at_y(d),
            )
            c.start()
            row.append(c)
        y_copies.append(row)
    pl.semaphore_wait(know_b, 2)
    for d in (4, -4):
        signal(know_c, at_z(d))

    def piece(i, k):
        b = blocks[i]
        owner = (FIRST + b * OWN + k) % NZ
        copy = remote(
            zbuf.at[b, k], zrecv.at[z], zs_sem.at[i, k], zr_sem.at[z], (owner * NY + y, sec)
        )
        return owner != z, copy

    for i, b in enumerate(blocks):
        for c in y_copies[i]:
            c.wait_recv()
        total = pbuf[y, b].astype(jnp.float32)
        for d in range(1, NY):
            total = total + yrecv[d - 1, b].astype(jnp.float32)
        zbuf[b] = total.astype(jnp.bfloat16)
        if i == 0:
            pl.semaphore_wait(know_c, 2)
        for k in range(OWN):
            other, c = piece(i, k)
            pl.when(other)(c.start)

    def spread(s):
        part = quarter.at[mb, mk]
        return remote(part, part, gs_sem.at[s], gr_sem.at[mb, mk], (s * NY + y, sec))

    @pl.when(is_owner)
    def _():
        total = zbuf[mb, mk].astype(jnp.float32)
        for d in NEAR_FIRST:
            s = (z + d) % NZ
            remote(zbuf.at[0, 0], zrecv.at[s], zs_sem.at[0, 0], zr_sem.at[s], at_z(1)).wait_recv()
            total = total + zrecv[s].astype(jnp.float32)
        quarter[mb, mk] = total.astype(jnp.bfloat16)
        for s in SPREAD:
            pl.when(s != z)(spread(s).start)

    h_copies = []
    for i, b in reversed(list(enumerate(blocks))):
        for k in range(OWN):
            part = quarter.at[b, k]
            arrival = remote(part, part, gs_sem.at[0], gr_sem.at[b, k], at_z(1))
            pl.when(b * OWN + k != mine)(arrival.wait_recv)
        for d in Y_FIRST:
            c = remote(
                quarter.at[b], out.at[y, b], hs_sem.at[d - 1, b], hr_sem.at[d - 1, b], at_y(d)
            )
            c.start()
            h_copies.append(c)
        c = pltpu.make_async_copy(quarter.at[b], out.at[y, b], out_sem.at[b])
        c.start()
        h_copies.append(c)

    for p in range(len(PARTS)):
        pl.when(has_up)(up[p].wait_send)
        pl.when(has_down)(down[p].wait_send)
    for row in y_copies:
        for c in row:
            c.wait_send()
    for i in range(NB):
        for k in range(OWN):
            other, c = piece(i, k)
            pl.when(other)(c.wait_send)

    @pl.when(is_owner)
    def _():
        for s in SPREAD:
            pl.when(s != z)(spread(s).wait_send)

    for c in h_copies:
        c.wait()


def local(psi, left_ops, right_ops, term_src, term_count):
    hbm = pl.BlockSpec(memory_space=pl.ANY)
    dma, plain = pltpu.SemaphoreType.DMA, pltpu.SemaphoreType.REGULAR
    bf16 = jnp.bfloat16
    out = pl.pallas_call(
        kernel,
        out_shape=jax.ShapeDtypeStruct((NY, NB, OWN, ROWS, M), bf16),
        in_specs=[hbm, hbm, hbm, hbm, hbm],
        out_specs=hbm,
        scratch_shapes=[
            pltpu.SMEM((SLOTS,), jnp.int32),
            pltpu.SMEM((1, 1), jnp.int32),
            *(pltpu.VMEM((3, rows, M), bf16) for first, rows in PARTS),
            pltpu.VMEM((M, SLOTS * M), bf16),
            pltpu.VMEM((SLOTS, M, M), bf16),
            pltpu.VMEM((SLOTS * M, M), bf16),
            pltpu.VMEM((M, M), jnp.float32),
            pltpu.VMEM((NY, NB, OWN, ROWS, M), bf16),
            pltpu.VMEM((NY - 1, NB, OWN, ROWS, M), bf16),
            pltpu.VMEM((NB, OWN, ROWS, M), bf16),
            pltpu.VMEM((NZ, ROWS, M), bf16),
            pltpu.VMEM((NB, OWN, ROWS, M), bf16),
            dma((2,)), dma((2, SLOTS)), dma((SLOTS,)), dma((2, 2)), dma((2, 2)),
            dma((NY - 1, NB)), dma((NY - 1, NB)),
            dma((NB, OWN)), dma((NZ,)),
            dma((NZ,)), dma((NB, OWN)),
            dma((NY - 1, NB)), dma((NY - 1, NB)), dma((NB,)),
            plain, plain, plain, dma((2,)),
        ],
        compiler_params=pltpu.CompilerParams(
            collective_id=0, has_side_effects=True, vmem_limit_bytes=60 * 1024 * 1024
        ),
        cost_estimate=pl.CostEstimate(
            flops=4 * SLOTS * M**3, bytes_accessed=4 * SLOTS * M * M, transcendentals=0
        ),
        name="sigma_sum",
    )(psi, left_ops, right_ops, term_src, term_count)
    return out.reshape(1, M, M)


def solution(mesh):
    in_specs = (
        P("sec", None, None),
        P(("op", "sec"), None, None),
        P(("op", "sec"), None, None),
        P(("op", "sec")),
        P("op", "sec"),
    )
    out_specs = P("sec", None, None)
    return jax.shard_map(local, mesh=mesh, in_specs=in_specs, out_specs=out_specs, check_vma=False)
```

```python
import jax
import jax.numpy as jnp
from jax import lax
from jax.experimental import pallas as pl
from jax.experimental.pallas import tpu as pltpu
from jax.sharding import PartitionSpec as P

MESH = pl.DeviceIdType.MESH
NY, NZ, NSEC = 4, 16, 8
M, SLOTS = 384, 7
PARTS = ((0, 256), (256, 128))
NB, OWN, ROWS, FIRST = 4, 3, 8, 10
NEAR_FIRST = (1, 15, 2, 14, 3, 13, 4, 12, 5, 11, 6, 10, 7, 9, 8)
FAR_BLOCKS = (
    (3, 2, 1, 0), (3, 2, 0, 1), (0, 3, 1, 2), (0, 1, 2, 3), (1, 0, 2, 3), (1, 2, 0, 3), (2, 1, 3, 0), (2, 3, 1, 0),
)
SPREAD = (0, 1, 2, 3, 4, 5, 6, 7, 15, 14, 13, 12, 8, 11, 9, 10)
Y_FIRST = (2, 1, 3)


def kernel(
    psi, left, right, src_in, count_in, out, src, count,
    near_a, near_b, lbuf, rbuf, icat, acc, pbuf, yrecv, zbuf, zrecv, quarter,
    psi_sem, l_sem, r_sem, psi_send, psi_recv,
    ys_sem, yr_sem, zs_sem, zr_sem, gs_sem, gr_sem, hs_sem, hr_sem, out_sem,
    know_a, know_b, know_c, scalar_sem,
):
    op, sec = lax.axis_index("op"), lax.axis_index("sec")
    z, y = op // NY, op % NY
    mine = (z + NZ - FIRST) % NZ
    is_owner = mine < NB * OWN
    mb, mk = mine // OWN % NB, mine % OWN
    group = jnp.where(is_owner, mine // OWN, mine - NB * OWN + NB)
    blocks = []
    for i in range(NB):
        block = FAR_BLOCKS[0][i]
        for g in range(1, 2 * NB):
            block = jnp.where(group == g, FAR_BLOCKS[g][i], block)
        blocks.append(block)

    def at_y(d):
        return (z * NY + (y + d) % NY, sec)

    def at_z(d):
        return ((z + d) % NZ * NY + y, sec)

    def at_sec(d):
        return (op, (sec + d) % NSEC)

    def remote(a, b, s, r, device):
        return pltpu.make_async_remote_copy(
            src_ref=a, dst_ref=b, send_sem=s, recv_sem=r,
            device_id=device, device_id_type=MESH,
        )

    def signal(sem, device):
        pl.semaphore_signal(sem, inc=1, device_id=device, device_id_type=MESH)

    barrier = pltpu.get_barrier_semaphore()
    beside = [at_z(1), at_z(-1), at_y(1), at_y(-1)]
    for peer in beside:
        signal(barrier, peer)
    has_up, has_down = sec < NSEC - 1, sec > 0

    @pl.when(has_up)
    def _():
        signal(barrier, at_sec(1))

    @pl.when(has_down)
    def _():
        signal(barrier, at_sec(-1))

    near = (near_a, near_b)
    own = [
        pltpu.make_async_copy(psi.at[0, pl.ds(*part)], near[p].at[1], psi_sem.at[p])
        for p, part in enumerate(PARTS)
    ]
    for c in own:
        c.start()
    loads = [
        pltpu.make_async_copy(src_in, src, scalar_sem.at[0]),
        pltpu.make_async_copy(count_in, count, scalar_sem.at[1]),
    ]
    for t in range(SLOTS):
        loads.append(pltpu.make_async_copy(right.at[t], rbuf.at[t], r_sem.at[t]))
    for p, (first, rows) in enumerate(PARTS):
        for t in range(SLOTS):
            loads.append(pltpu.make_async_copy(
                left.at[t, :, pl.ds(first, rows)],
                lbuf.at[:, pl.ds(SLOTS * first + t * rows, rows)],
                l_sem.at[p, t],
            ))

    ends = ((sec == 0) | (sec == NSEC - 1)).astype(jnp.int32)
    pl.semaphore_wait(barrier, 6 - ends)
    for c in own:
        c.wait()
    even = sec % 2 == 0
    up, down, fill_low, fill_high = [], [], [], []
    for p, part in enumerate(PARTS):
        rows, held = pl.ds(*part), near[p]
        up.append(remote(held.at[1], held.at[0], psi_send.at[p, 0], psi_recv.at[p, 0], at_sec(1)))
        down.append(remote(held.at[1], held.at[2], psi_send.at[p, 1], psi_recv.at[p, 1], at_sec(-1)))
        fill_low.append(pltpu.make_async_copy(psi.at[0, rows], held.at[0], psi_recv.at[p, 0]))
        fill_high.append(pltpu.make_async_copy(psi.at[0, rows], held.at[2], psi_recv.at[p, 1]))
    for p in range(len(PARTS)):
        pl.when(even & has_down)(down[p].start)
        pl.when(jnp.logical_not(even) & has_up)(up[p].start)
    for p in range(len(PARTS)):
        pl.when(even)(up[p].start)
        pl.when(jnp.logical_not(even))(down[p].start)
        pl.when(sec == 0)(fill_low[p].start)
        pl.when(sec == NSEC - 1)(fill_high[p].start)
    for peer in beside:
        signal(know_a, peer)
    for c in loads:
        c.start()
    pl.semaphore_wait(know_a, 4)
    for d in (2, -2):
        signal(know_b, at_z(d))
    for c in loads:
        c.wait()

    live = count[0, 0]
    for p, (first, rows) in enumerate(PARTS):
        pl.when(has_down)(up[p].wait_recv)
        pl.when(has_up)(down[p].wait_recv)
        pl.when(sec == 0)(fill_low[p].wait)
        pl.when(sec == NSEC - 1)(fill_high[p].wait)
        if p == 1:
            pl.semaphore_wait(know_b, 2)
            for d in (4, -4):
                signal(know_c, at_z(d))
        for t in range(SLOTS):
            block = near[p][jnp.clip(src[t] - sec + 1, 0, 2)]
            inner = jnp.dot(block, rbuf[t], preferred_element_type=jnp.float32)
            inner = jnp.where(t < live, inner, 0.0).astype(jnp.bfloat16)
            icat[pl.ds(SLOTS * first + t * rows, rows)] = inner
        span = pl.ds(SLOTS * first, SLOTS * rows)
        term = jnp.dot(lbuf[:, span], icat[span], preferred_element_type=jnp.float32)
        if p == 0:
            acc[...] = term
    total = acc[...] + term
    pbuf[...] = total.astype(jnp.bfloat16).reshape(NY, NB, OWN, ROWS, M)

    y_copies = []
    for i, b in enumerate(blocks):
        row = []
        for d in Y_FIRST:
            c = remote(
                pbuf.at[(y + d) % NY, b], yrecv.at[d - 1, b],
                ys_sem.at[d - 1, i], yr_sem.at[d - 1, i], at_y(d),
            )
            c.start()
            row.append(c)
        y_copies.append(row)

    def piece(i, k):
        b = blocks[i]
        owner = (FIRST + b * OWN + k) % NZ
        copy = remote(
            zbuf.at[b, k], zrecv.at[z], zs_sem.at[i, k], zr_sem.at[z], (owner * NY + y, sec)
        )
        return owner != z, copy

    for i, b in enumerate(blocks):
        for c in y_copies[i]:
            c.wait_recv()
        total = pbuf[y, b].astype(jnp.float32)
        for d in range(1, NY):
            total = total + yrecv[d - 1, b].astype(jnp.float32)
        zbuf[b] = total.astype(jnp.bfloat16)
        if i == 0:
            pl.semaphore_wait(know_c, 2)
        for k in range(OWN):
            other, c = piece(i, k)
            pl.when(other)(c.start)

    def spread(s):
        part = quarter.at[mb, mk]
        return remote(part, part, gs_sem.at[s], gr_sem.at[mb, mk], (s * NY + y, sec))

    @pl.when(is_owner)
    def _():
        total = zbuf[mb, mk].astype(jnp.float32)
        for d in NEAR_FIRST:
            s = (z + d) % NZ
            remote(zbuf.at[0, 0], zrecv.at[s], zs_sem.at[0, 0], zr_sem.at[s], at_z(1)).wait_recv()
            total = total + zrecv[s].astype(jnp.float32)
        quarter[mb, mk] = total.astype(jnp.bfloat16)
        for s in SPREAD:
            pl.when(s != z)(spread(s).start)

    h_copies = []
    for i, b in reversed(list(enumerate(blocks))):
        for k in range(OWN):
            part = quarter.at[b, k]
            arrival = remote(part, part, gs_sem.at[0], gr_sem.at[b, k], at_z(1))
            pl.when(b * OWN + k != mine)(arrival.wait_recv)
        for d in Y_FIRST:
            c = remote(
                quarter.at[b], out.at[y, b], hs_sem.at[d - 1, b], hr_sem.at[d - 1, b], at_y(d)
            )
            c.start()
            h_copies.append(c)
        c = pltpu.make_async_copy(quarter.at[b], out.at[y, b], out_sem.at[b])
        c.start()
        h_copies.append(c)

    for p in range(len(PARTS)):
        pl.when(has_up)(up[p].wait_send)
        pl.when(has_down)(down[p].wait_send)
    for row in y_copies:
        for c in row:
            c.wait_send()
    for i in range(NB):
        for k in range(OWN):
            other, c = piece(i, k)
            pl.when(other)(c.wait_send)

    @pl.when(is_owner)
    def _():
        for s in SPREAD:
            pl.when(s != z)(spread(s).wait_send)

    for c in h_copies:
        c.wait()


def local(psi, left_ops, right_ops, term_src, term_count):
    hbm = pl.BlockSpec(memory_space=pl.ANY)
    dma, plain = pltpu.SemaphoreType.DMA, pltpu.SemaphoreType.REGULAR
    bf16 = jnp.bfloat16
    out = pl.pallas_call(
        kernel,
        out_shape=jax.ShapeDtypeStruct((NY, NB, OWN, ROWS, M), bf16),
        in_specs=[hbm, hbm, hbm, hbm, hbm],
        out_specs=hbm,
        scratch_shapes=[
            pltpu.SMEM((SLOTS,), jnp.int32),
            pltpu.SMEM((1, 1), jnp.int32),
            *(pltpu.VMEM((3, rows, M), bf16) for first, rows in PARTS),
            pltpu.VMEM((M, SLOTS * M), bf16),
            pltpu.VMEM((SLOTS, M, M), bf16),
            pltpu.VMEM((SLOTS * M, M), bf16),
            pltpu.VMEM((M, M), jnp.float32),
            pltpu.VMEM((NY, NB, OWN, ROWS, M), bf16),
            pltpu.VMEM((NY - 1, NB, OWN, ROWS, M), bf16),
            pltpu.VMEM((NB, OWN, ROWS, M), bf16),
            pltpu.VMEM((NZ, ROWS, M), bf16),
            pltpu.VMEM((NB, OWN, ROWS, M), bf16),
            dma((2,)), dma((2, SLOTS)), dma((SLOTS,)), dma((2, 2)), dma((2, 2)),
            dma((NY - 1, NB)), dma((NY - 1, NB)),
            dma((NB, OWN)), dma((NZ,)),
            dma((NZ,)), dma((NB, OWN)),
            dma((NY - 1, NB)), dma((NY - 1, NB)), dma((NB,)),
            plain, plain, plain, dma((2,)),
        ],
        compiler_params=pltpu.CompilerParams(
            collective_id=0, has_side_effects=True, vmem_limit_bytes=60 * 1024 * 1024
        ),
        cost_estimate=pl.CostEstimate(
            flops=4 * SLOTS * M**3, bytes_accessed=4 * SLOTS * M * M, transcendentals=0
        ),
        name="sigma_sum",
    )(psi, left_ops, right_ops, term_src, term_count)
    return out.reshape(1, M, M)


def solution(mesh):
    in_specs = (
        P("sec", None, None),
        P(("op", "sec"), None, None),
        P(("op", "sec"), None, None),
        P(("op", "sec")),
        P("op", "sec"),
    )
    out_specs = P("sec", None, None)
    return jax.shard_map(local, mesh=mesh, in_specs=in_specs, out_specs=out_specs, check_vma=False)
```

```python
import jax
import jax.numpy as jnp
from jax import lax
from jax.experimental import pallas as pl
from jax.experimental.pallas import tpu as pltpu
from jax.sharding import PartitionSpec as P

MESH = pl.DeviceIdType.MESH
NY, NZ, NSEC = 4, 16, 8
M, SLOTS = 384, 7
PARTS = ((0, 256), (256, 128))
NB, OWN, ROWS, FIRST = 4, 3, 8, 10
NEAR_FIRST = (1, 15, 2, 14, 3, 13, 4, 12, 5, 11, 6, 10, 7, 9, 8)
FAR_BLOCKS = (
    (3, 2, 1, 0), (3, 2, 0, 1), (0, 3, 1, 2), (0, 1, 2, 3), (1, 0, 2, 3), (1, 2, 0, 3), (2, 1, 3, 0), (2, 3, 1, 0),
)
SPREAD = (0, 1, 2, 3, 4, 5, 6, 7, 15, 14, 13, 12, 8, 11, 9, 10)
Y_FIRST = (2, 1, 3)


def kernel(
    psi, left, right, src_in, count_in, out, src, count,
    near_a, near_b, lbuf, rbuf, icat, acc, pbuf, yrecv, zbuf, zrecv, quarter,
    psi_sem, l_sem, r_sem, psi_send, psi_recv,
    ys_sem, yr_sem, zs_sem, zr_sem, gs_sem, gr_sem, hs_sem, hr_sem, out_sem,
    know_a, know_b, know_c, scalar_sem, fs_sem, fr_sem,
):
    op, sec = lax.axis_index("op"), lax.axis_index("sec")
    z, y = op // NY, op % NY
    mine = (z + NZ - FIRST) % NZ
    is_owner = mine < NB * OWN
    mb, mk = mine // OWN % NB, mine % OWN
    group = jnp.where(is_owner, mine // OWN, mine - NB * OWN + NB)
    blocks = []
    for i in range(NB):
        block = FAR_BLOCKS[0][i]
        for g in range(1, 2 * NB):
            block = jnp.where(group == g, FAR_BLOCKS[g][i], block)
        blocks.append(block)

    def at_y(d):
        return (z * NY + (y + d) % NY, sec)

    def at_z(d):
        return ((z + d) % NZ * NY + y, sec)

    def at_sec(d):
        return (op, (sec + d) % NSEC)

    def remote(a, b, s, r, device):
        return pltpu.make_async_remote_copy(
            src_ref=a, dst_ref=b, send_sem=s, recv_sem=r,
            device_id=device, device_id_type=MESH,
        )

    def signal(sem, device):
        pl.semaphore_signal(sem, inc=1, device_id=device, device_id_type=MESH)

    barrier = pltpu.get_barrier_semaphore()
    beside = [at_z(1), at_z(-1), at_y(1), at_y(-1)]
    for peer in beside:
        signal(barrier, peer)
    has_up, has_down = sec < NSEC - 1, sec > 0

    @pl.when(has_up)
    def _():
        signal(barrier, at_sec(1))

    @pl.when(has_down)
    def _():
        signal(barrier, at_sec(-1))

    near = (near_a, near_b)
    own = [
        pltpu.make_async_copy(psi.at[0, pl.ds(*part)], near[p].at[1], psi_sem.at[p])
        for p, part in enumerate(PARTS)
    ]
    for c in own:
        c.start()
    loads = [
        pltpu.make_async_copy(src_in, src, scalar_sem.at[0]),
        pltpu.make_async_copy(count_in, count, scalar_sem.at[1]),
    ]
    for t in range(SLOTS):
        loads.append(pltpu.make_async_copy(right.at[t], rbuf.at[t], r_sem.at[t]))
    for p, (first, rows) in enumerate(PARTS):
        for t in range(SLOTS):
            loads.append(pltpu.make_async_copy(
                left.at[t, :, pl.ds(first, rows)],
                lbuf.at[:, pl.ds(SLOTS * first + t * rows, rows)],
                l_sem.at[p, t],
            ))

    ends = ((sec == 0) | (sec == NSEC - 1)).astype(jnp.int32)
    pl.semaphore_wait(barrier, 6 - ends)
    for c in own:
        c.wait()
    even = sec % 2 == 0
    up, down, fill_low, fill_high = [], [], [], []
    for p, part in enumerate(PARTS):
        rows, held = pl.ds(*part), near[p]
        up.append(remote(held.at[1], held.at[0], psi_send.at[p, 0], psi_recv.at[p, 0], at_sec(1)))
        down.append(remote(held.at[1], held.at[2], psi_send.at[p, 1], psi_recv.at[p, 1], at_sec(-1)))
        fill_low.append(pltpu.make_async_copy(psi.at[0, rows], held.at[0], psi_recv.at[p, 0]))
        fill_high.append(pltpu.make_async_copy(psi.at[0, rows], held.at[2], psi_recv.at[p, 1]))
    for p in range(len(PARTS)):
        pl.when(even & has_down)(down[p].start)
        pl.when(jnp.logical_not(even) & has_up)(up[p].start)
    for p in range(len(PARTS)):
        pl.when(even)(up[p].start)
        pl.when(jnp.logical_not(even))(down[p].start)
        pl.when(sec == 0)(fill_low[p].start)
        pl.when(sec == NSEC - 1)(fill_high[p].start)
    for peer in beside:
        signal(know_a, peer)
    for c in loads:
        c.start()
    pl.semaphore_wait(know_a, 4)
    for d in (2, -2):
        signal(know_b, at_z(d))
    for c in loads:
        c.wait()

    live = count[0, 0]
    for p, (first, rows) in enumerate(PARTS):
        pl.when(has_down)(up[p].wait_recv)
        pl.when(has_up)(down[p].wait_recv)
        pl.when(sec == 0)(fill_low[p].wait)
        pl.when(sec == NSEC - 1)(fill_high[p].wait)
        if p == 1:
            pl.semaphore_wait(know_b, 2)
            for d in (4, -4):
                signal(know_c, at_z(d))
        for t in range(SLOTS):
            block = near[p][jnp.clip(src[t] - sec + 1, 0, 2)]
            inner = jnp.dot(block, rbuf[t], preferred_element_type=jnp.float32)
            inner = jnp.where(t < live, inner, 0.0).astype(jnp.bfloat16)
            icat[pl.ds(SLOTS * first + t * rows, rows)] = inner
        span = pl.ds(SLOTS * first, SLOTS * rows)
        term = jnp.dot(lbuf[:, span], icat[span], preferred_element_type=jnp.float32)
        if p == 0:
            acc[...] = term
    total = acc[...] + term
    pbuf[...] = total.astype(jnp.bfloat16).reshape(NY, NB, OWN, ROWS, M)

    y_copies = []
    for i, b in enumerate(blocks):
        row = []
        for d in Y_FIRST:
            c = remote(
                pbuf.at[(y + d) % NY, b], yrecv.at[d - 1, b],
                ys_sem.at[d - 1, i], yr_sem.at[d - 1, i], at_y(d),
            )
            c.start()
            row.append(c)
        y_copies.append(row)

    def piece(i, k):
        b = blocks[i]
        owner = (FIRST + b * OWN + k) % NZ
        copy = remote(
            zbuf.at[b, k], zrecv.at[z], zs_sem.at[i, k], zr_sem.at[z], (owner * NY + y, sec)
        )
        return owner != z, copy

    for i, b in enumerate(blocks):
        for c in y_copies[i]:
            c.wait_recv()
        total = pbuf[y, b].astype(jnp.float32)
        for d in range(1, NY):
            total = total + yrecv[d - 1, b].astype(jnp.float32)
        zbuf[b] = total.astype(jnp.bfloat16)
        if i == 0:
            pl.semaphore_wait(know_c, 2)
        for k in range(OWN):
            other, c = piece(i, k)
            pl.when(other)(c.start)

    def spread(s):
        part = quarter.at[mb, mk]
        return remote(part, part, gs_sem.at[s], gr_sem.at[mb, mk], (s * NY + y, sec))

    @pl.when(is_owner)
    def _():
        total = zbuf[mb, mk].astype(jnp.float32)
        for d in NEAR_FIRST:
            s = (z + d) % NZ
            remote(zbuf.at[0, 0], zrecv.at[s], zs_sem.at[0, 0], zr_sem.at[s], at_z(1)).wait_recv()
            total = total + zrecv[s].astype(jnp.float32)
        quarter[mb, mk] = total.astype(jnp.bfloat16)
        for s in SPREAD:
            pl.when(s != z)(spread(s).start)

    h_copies = []
    for i, b in reversed(list(enumerate(blocks))):
        for k in range(OWN):
            part = quarter.at[b, k]
            arrival = remote(part, part, gs_sem.at[0], gr_sem.at[b, k], at_z(1))
            pl.when(b * OWN + k != mine)(arrival.wait_recv)
            if i == 0:
                for d in Y_FIRST:
                    c = remote(
                        part, out.at[y, b, k], fs_sem.at[d - 1, k], fr_sem.at[d - 1, k], at_y(d)
                    )
                    c.start()
                    h_copies.append(c)
        for d in Y_FIRST if i else ():
            c = remote(
                quarter.at[b], out.at[y, b], hs_sem.at[d - 1, b], hr_sem.at[d - 1, b], at_y(d)
            )
            c.start()
            h_copies.append(c)
        c = pltpu.make_async_copy(quarter.at[b], out.at[y, b], out_sem.at[b])
        c.start()
        h_copies.append(c)

    for p in range(len(PARTS)):
        pl.when(has_up)(up[p].wait_send)
        pl.when(has_down)(down[p].wait_send)
    for row in y_copies:
        for c in row:
            c.wait_send()
    for i in range(NB):
        for k in range(OWN):
            other, c = piece(i, k)
            pl.when(other)(c.wait_send)

    @pl.when(is_owner)
    def _():
        for s in SPREAD:
            pl.when(s != z)(spread(s).wait_send)

    for c in h_copies:
        c.wait()


def local(psi, left_ops, right_ops, term_src, term_count):
    hbm = pl.BlockSpec(memory_space=pl.ANY)
    dma, plain = pltpu.SemaphoreType.DMA, pltpu.SemaphoreType.REGULAR
    bf16 = jnp.bfloat16
    out = pl.pallas_call(
        kernel,
        out_shape=jax.ShapeDtypeStruct((NY, NB, OWN, ROWS, M), bf16),
        in_specs=[hbm, hbm, hbm, hbm, hbm],
        out_specs=hbm,
        scratch_shapes=[
            pltpu.SMEM((SLOTS,), jnp.int32),
            pltpu.SMEM((1, 1), jnp.int32),
            *(pltpu.VMEM((3, rows, M), bf16) for first, rows in PARTS),
            pltpu.VMEM((M, SLOTS * M), bf16),
            pltpu.VMEM((SLOTS, M, M), bf16),
            pltpu.VMEM((SLOTS * M, M), bf16),
            pltpu.VMEM((M, M), jnp.float32),
            pltpu.VMEM((NY, NB, OWN, ROWS, M), bf16),
            pltpu.VMEM((NY - 1, NB, OWN, ROWS, M), bf16),
            pltpu.VMEM((NB, OWN, ROWS, M), bf16),
            pltpu.VMEM((NZ, ROWS, M), bf16),
            pltpu.VMEM((NB, OWN, ROWS, M), bf16),
            dma((2,)), dma((2, SLOTS)), dma((SLOTS,)), dma((2, 2)), dma((2, 2)),
            dma((NY - 1, NB)), dma((NY - 1, NB)),
            dma((NB, OWN)), dma((NZ,)),
            dma((NZ,)), dma((NB, OWN)),
            dma((NY - 1, NB)), dma((NY - 1, NB)), dma((NB,)),
            plain, plain, plain, dma((2,)), dma((NY - 1, OWN)), dma((NY - 1, OWN)),
        ],
        compiler_params=pltpu.CompilerParams(
            collective_id=0, has_side_effects=True, vmem_limit_bytes=60 * 1024 * 1024
        ),
        cost_estimate=pl.CostEstimate(
            flops=4 * SLOTS * M**3, bytes_accessed=4 * SLOTS * M * M, transcendentals=0
        ),
        name="sigma_sum",
    )(psi, left_ops, right_ops, term_src, term_count)
    return out.reshape(1, M, M)


def solution(mesh):
    in_specs = (
        P("sec", None, None),
        P(("op", "sec"), None, None),
        P(("op", "sec"), None, None),
        P(("op", "sec")),
        P("op", "sec"),
    )
    out_specs = P("sec", None, None)
    return jax.shard_map(local, mesh=mesh, in_specs=in_specs, out_specs=out_specs, check_vma=False)
```
